256 devices in a mesh: blk: 32 (over x_lo, z, core), tp: 8 (over y, x_hi).
Axes of the slice: x: 4 (x_hi: 2, x_lo: 2; x = x_hi * 2 + x_lo), y: 4, z: 8, core: 2. Of those that a mesh axis runs over, the one named last changes fastest.
Arguments:
- step_index: int32 [1], replicated, may hold values from 0 to 999
- patch_ids: int32 [32, 2, 512], P('blk'), may hold values from 0 to 255
- noisy_pool: bfloat16 [8192, 2048], P('blk'), may hold values from -6 to 6
- clean_pool: bfloat16 [8192, 2048], P('blk'), may hold values from -6 to 6
- norm_gain: bfloat16 [2048], replicated, may hold values from 0.099609375 to 1.8984375
- q_weight: bfloat16 [2048, 2048], P(None, 'tp'), may hold values from -480 to 480
- k_weight: bfloat16 [2048, 2048], P(None, 'tp'), may hold values from -6 to 6
- value_weight: bfloat16 [65536, 2048], P('blk', 'tp'), may hold values from -6 to 6
- out_weight: bfloat16 [65536, 2048], P(('blk', 'tp')), may hold values from -6 to 6
- value_m: bfloat16 [65536, 2048], P('blk', 'tp'), may hold values from -1.5 to 1.5
- value_v: bfloat16 [65536, 2048], P('blk', 'tp'), may hold values from 0.0009994507 to 0.099609375
- out_m: bfloat16 [65536, 2048], P(('blk', 'tp')), may hold values from -1.5 to 1.5
- out_v: bfloat16 [65536, 2048], P(('blk', 'tp')), may hold values from 0.0009994507 to 0.099609375
Outputs:
- new_value_weight: bfloat16 [65536, 2048], P('blk', 'tp')
- new_out_weight: bfloat16 [65536, 2048], P(('blk', 'tp'))
- token_loss: float32 [64, 512], P('blk', 'tp')
The draws below stay inside these ranges and needn't reach their ends.
Inputs may be any that keep to these rules, and one draw needn't show every extreme that they name: `patch_ids`: row numbers within the replica's own block of pool rows.
All inputs are finite; a program needn't handle non-finite values.
Results may differ from the reference program's by a relative error of at most 0.0086.
The reference program's roundings to bfloat16 on the way count: a program that leaves them out, or rounds other values in their place, can miss the bound.
Values may be sent and summed in bfloat16 or wider, within the bound.
A program may use at most 128 MiB of HBM per device.

```python
import math
import jax
import jax.numpy as jnp
from jax import lax

D = 2048
HEADS = 16
HEAD = 128
TOK = 512
POOL = 256
STEPS = 2
INNER = 2048
REPLICAS = 32
N_BLK = 32
N_TP = 8


def draw_q_weight(key, part):
    first_key = jax.random.fold_in(jax.random.fold_in(key, 17), 0)
    base = jax.random.truncated_normal(first_key, -6.0, 6.0, (D, INNER), jnp.float32)
    return (base * 3.0).astype(jnp.bfloat16)


def plant(entries, rng, smallest, top_value):
    index_at = [jax.random.randint(jax.random.fold_in(rng, axis), (), 0, length) for axis, length in enumerate(entries.shape)]
    longest = entries.shape.index(max(entries.shape))
    neighbour = index_at[:longest] + [(index_at[longest] + 1) % entries.shape[longest]] + index_at[longest + 1:]
    return entries.at[tuple(index_at)].set(smallest).at[tuple(neighbour)].set(top_value)


def shard_levels(stream_key, extent, cuts, smallest, high):
    level = 1.0
    for dim, shards_of in cuts:
        heights = jax.random.uniform(jax.random.fold_in(jax.random.fold_in(stream_key, 6), dim), (shards_of,), jnp.float32, smallest / len(cuts), high / len(cuts))
        level = level * jnp.repeat(jnp.exp(heights), extent[dim] // shards_of).reshape((-1,) + (1,) * (len(extent) - 1 - dim))
    return level


def bell_draw(own_key, shape, scale, reach, pieces=(), held_as=jnp.bfloat16):
    drawn = scale * jax.random.normal(own_key, shape, jnp.float32)
    if pieces:
        drawn = drawn * shard_levels(own_key, shape, pieces, -0.22, 0.18)
    return jnp.clip(drawn, -reach, reach).astype(held_as)


def setup_inputs(seed: int = 0) -> dict:
    seeds = jax.random.split(jax.random.key(seed), 14)
    step_index = jax.random.randint(seeds[0], (1,), 0, 1000).astype(jnp.int32)
    patch_ids = plant(jax.random.randint(seeds[1], (REPLICAS, STEPS, TOK), 0, POOL), jax.random.fold_in(seeds[1], 1), 0, POOL - 1).astype(jnp.int32)
    noisy_pool = bell_draw(seeds[2], (REPLICAS * POOL, D), 1.0, 6.0, ((0, 32),))
    clean_pool = bell_draw(seeds[3], (REPLICAS * POOL, D), 1.0, 6.0, ((0, 32),))
    norm_gain = jnp.clip(1.0 + 0.18 * jax.random.normal(seeds[4], (D,), jnp.float32), 0.099609375, 1.8984375).astype(jnp.bfloat16)
    q_weight = draw_q_weight(jax.random.fold_in(seeds[13], 71), 0)
    k_weight = bell_draw(seeds[6], (D, INNER), 1.0, 6.0, ((1, 8),))
    value_weight = bell_draw(seeds[7], (REPLICAS * D, INNER), 1.0, 6.0, ((0, 32), (1, 8)))
    out_weight = bell_draw(seeds[8], (REPLICAS * INNER, D), 1.0, 6.0, ((0, 256),))
    value_m = bell_draw(seeds[9], (REPLICAS * D, INNER), 0.1, 1.5, ((0, 32), (1, 8)))
    value_v = jnp.clip(jnp.exp(math.log(0.099609375) - 4.6018058 * jax.random.uniform(seeds[10], (REPLICAS * D, INNER), jnp.float32) ** shard_levels(seeds[10], (REPLICAS * D, INNER), ((0, 32), (1, 8)), -0.2, 0.2)), 0.0009994507, 0.099609375).astype(jnp.bfloat16)
    out_m = bell_draw(seeds[11], (REPLICAS * INNER, D), 0.1, 1.5, ((0, 256),))
    out_v = jnp.clip(jnp.exp(math.log(0.099609375) - 4.6018058 * jax.random.uniform(seeds[12], (REPLICAS * INNER, D), jnp.float32) ** shard_levels(seeds[12], (REPLICAS * INNER, D), ((0, 256),), -0.2, 0.2)), 0.0009994507, 0.099609375).astype(jnp.bfloat16)
    return dict(step_index=step_index, patch_ids=patch_ids, noisy_pool=noisy_pool, clean_pool=clean_pool, norm_gain=norm_gain, q_weight=q_weight, k_weight=k_weight, value_weight=value_weight, out_weight=out_weight, value_m=value_m, value_v=value_v, out_m=out_m, out_v=out_v)


beta_one = 0.9
beta_two = 0.95
learn_rate = 0.05
decay_rate = 0.1
epsilon = 1e-08

def normalize(rows, gain):
    wide = rows.astype(jnp.float32)
    mean_sq = lax.optimization_barrier(jnp.mean(wide * wide, axis=-1, keepdims=True))
    return (wide * lax.rsqrt(mean_sq + 1e-05) * gain.astype(jnp.float32)).astype(jnp.bfloat16)

def adam_update(weight, peer, moment, second, grad):
    first = beta_one * moment.astype(jnp.float32) + (1.0 - beta_one) * grad
    square = beta_two * second.astype(jnp.float32) + (1.0 - beta_two) * grad * grad
    middle = 0.5 * (weight.astype(jnp.float32) + peer.astype(jnp.float32))
    updated = middle - learn_rate * (first / (jnp.sqrt(square) + epsilon) + decay_rate * middle)
    return (updated.astype(jnp.bfloat16), first.astype(jnp.bfloat16), square.astype(jnp.bfloat16))

def replica_step(normed, inputs, targets, q_weight, k_weight, value_w, out_w):
    in_scale = D ** (-0.5)
    out_scale = INNER ** (-0.5)
    queries = (jnp.dot(normed, q_weight, preferred_element_type=jnp.float32) * in_scale).astype(jnp.bfloat16)
    keys_all = (jnp.dot(normed, k_weight, preferred_element_type=jnp.float32) * in_scale).astype(jnp.bfloat16)
    values_all = (jnp.dot(normed, value_w, preferred_element_type=jnp.float32) * in_scale).astype(jnp.bfloat16)
    qh = queries.reshape(TOK, HEADS, HEAD).astype(jnp.float32)
    kh = keys_all.reshape(TOK, HEADS, HEAD).astype(jnp.float32)
    vh = values_all.reshape(TOK, HEADS, HEAD).astype(jnp.float32)
    scores = jnp.einsum('thd,shd->hts', qh, kh) * HEAD ** (-0.5)
    scores = scores - lax.optimization_barrier(jnp.max(scores, axis=-1, keepdims=True))
    weights = jnp.exp(scores)
    probs = (weights / lax.optimization_barrier(jnp.sum(weights, axis=-1, keepdims=True))).astype(jnp.bfloat16)
    mixed = jnp.einsum('hts,shd->thd', probs.astype(jnp.float32), vh).astype(jnp.bfloat16).reshape(TOK, INNER)
    group_w = INNER // N_TP
    mixed_g = mixed.reshape(TOK, N_TP, group_w).astype(jnp.float32)
    out_g = out_w.reshape(N_TP, group_w, D).astype(jnp.float32)
    partial_sums = (jnp.einsum('tgi,gid->gtd', mixed_g, out_g) * out_scale).astype(jnp.bfloat16)
    attn = lax.optimization_barrier(jnp.sum(partial_sums.astype(jnp.float32), axis=0))
    error = inputs.astype(jnp.float32) + attn - targets.astype(jnp.float32)
    token_err = lax.optimization_barrier(jnp.mean(error * error, axis=-1))
    grad_out = error.astype(jnp.bfloat16)
    grad_wo = jnp.dot(mixed.T, grad_out, preferred_element_type=jnp.float32) * out_scale
    grad_mixed = (jnp.dot(grad_out, out_w.T, preferred_element_type=jnp.float32) * out_scale).astype(jnp.bfloat16)
    gm = grad_mixed.reshape(TOK, HEADS, HEAD).astype(jnp.float32)
    grad_values = jnp.einsum('hts,thd->shd', probs.astype(jnp.float32), gm).astype(jnp.bfloat16).reshape(TOK, INNER)
    grad_wv = jnp.dot(normed.T, grad_values, preferred_element_type=jnp.float32) * in_scale
    return (token_err, grad_wv, grad_wo)

def reference(step_index, patch_ids, noisy_pool, clean_pool, norm_gain, q_weight, k_weight, value_weight, out_weight, value_m, value_v, out_m, out_v):
    nbits = N_BLK.bit_length() - 1
    noisy = noisy_pool.reshape(N_BLK, POOL, D)
    clean = clean_pool.reshape(N_BLK, POOL, D)
    value_w = value_weight.reshape(N_BLK, D, INNER)
    out_w = out_weight.reshape(N_BLK, INNER, D)
    vm = value_m.reshape(N_BLK, D, INNER)
    vv = value_v.reshape(N_BLK, D, INNER)
    om = out_m.reshape(N_BLK, INNER, D)
    ov = out_v.reshape(N_BLK, INNER, D)
    replica_rows = jnp.arange(N_BLK, dtype=jnp.int32)[:, None]
    losses = []
    for section in range(STEPS):
        ids = patch_ids[:, section, :].astype(jnp.int32)
        inputs = noisy[replica_rows, ids]
        targets = clean[replica_rows, ids]
        normed = normalize(inputs, norm_gain)

        def one(args):
            return replica_step(args[0], args[1], args[2], q_weight, k_weight, args[3], args[4])
        token_err, grad_wv, grad_wo = lax.map(one, (normed, inputs, targets, value_w, out_w))
        exponent = (step_index[0].astype(jnp.int32) + section) % nbits
        distance = jnp.left_shift(jnp.int32(1), exponent)
        peer_v = jnp.roll(value_w, distance, axis=0)
        peer_o = jnp.roll(out_w, distance, axis=0)
        value_w, vm, vv = adam_update(value_w, peer_v, vm, vv, grad_wv)
        out_w, om, ov = adam_update(out_w, peer_o, om, ov, grad_wo)
        losses.append(token_err)
    token_loss = jnp.stack(losses, axis=1).reshape(N_BLK * STEPS, TOK)
    return (value_w.reshape(N_BLK * D, INNER), out_w.reshape(N_BLK * INNER, D), token_loss)
```

```python
import functools

import jax
import jax.numpy as jnp
from jax import lax
from jax.sharding import PartitionSpec as P

D = 2048
HEAD = 128
STEPS = 2
INNER = 2048
POOL = 256

beta_one = 0.9
beta_two = 0.95
learn_rate = 0.05
decay_rate = 0.1
epsilon = 1e-08

BF = jnp.bfloat16
F32 = jnp.float32


def from_behind(block, axis, distance):
    n = lax.axis_size(axis)
    route = [((i - distance) % n, i) for i in range(n)]
    return lax.ppermute(block, axis, route)


def normalize(rows, gain):
    wide = rows.astype(F32)
    mean_sq = jnp.mean(wide * wide, axis=-1, keepdims=True)
    return (wide * lax.rsqrt(mean_sq + 1e-05) * gain.astype(F32)).astype(BF)


def adam_update(weight, peer, moment, second, grad):
    first = beta_one * moment.astype(F32) + (1.0 - beta_one) * grad
    square = beta_two * second.astype(F32) + (1.0 - beta_two) * grad * grad
    middle = 0.5 * (weight.astype(F32) + peer.astype(F32))
    updated = middle - learn_rate * (first / (jnp.sqrt(square) + epsilon) + decay_rate * middle)
    return (updated.astype(BF), first.astype(BF), square.astype(BF))


def dot(a, b):
    return jnp.dot(a, b, preferred_element_type=F32)


def weighted(rows, count):
    return (rows.astype(F32) * count[:, None]).astype(BF)


def body(start, patch_ids, noisy, clean, norm_gain, q_weight, k_weight, value_w, out_w, value_mom, value_sec, out_mom, out_sec):
    groups = lax.axis_size("tp")
    nbits = lax.axis_size("blk").bit_length() - 1
    rank = lax.axis_index("tp")
    share = patch_ids.shape[2] // groups
    inner_dev = q_weight.shape[1]
    heads = inner_dev // HEAD
    in_scale = D ** (-0.5)
    out_scale = INNER ** (-0.5)
    score_scale = HEAD ** (-0.5)
    normed = normalize(noisy, norm_gain)
    queries = (dot(normed, q_weight) * in_scale).astype(BF)
    keys = (dot(normed, k_weight) * in_scale).astype(BF)
    scores = [
        dot(queries[:, h * HEAD : (h + 1) * HEAD], keys[:, h * HEAD : (h + 1) * HEAD].T) * score_scale
        for h in range(heads)
    ]
    losses = []
    for section in range(STEPS):
        distance = 1 << ((start + section) % nbits)
        peer_v = from_behind(value_w, "blk", distance)
        peer_o = from_behind(out_w, "blk", distance)
        ids = patch_ids[0, section]
        count = jnp.sum((ids[:, None] == jnp.arange(POOL)[None, :]).astype(F32), axis=0)
        probs = []
        for sc in scores:
            sc = jnp.where(count[None, :] > 0, sc, -jnp.inf)
            e = jnp.exp(sc - jnp.max(sc, axis=-1, keepdims=True))
            probs.append((e / jnp.sum(e * count[None, :], axis=-1, keepdims=True)).astype(BF))
        values = (dot(normed, value_w) * in_scale).astype(BF)
        values_c = weighted(values, count)
        mixed = jnp.concatenate(
            [dot(probs[h], values_c[:, h * HEAD : (h + 1) * HEAD]) for h in range(heads)], axis=1
        ).astype(BF)
        partial_out = (dot(mixed, out_w) * out_scale).astype(BF)
        summed = lax.psum(partial_out, "tp").astype(F32)
        error = noisy.astype(F32) + summed - clean.astype(F32)
        token_err = jnp.mean(error * error, axis=-1)
        mine = lax.dynamic_slice_in_dim(ids, rank * share, share, 0)
        losses.append(jnp.sum(jnp.where(mine[:, None] == jnp.arange(POOL)[None, :], token_err[None, :], 0.0), axis=1))
        grad_out = error.astype(BF)
        grad_wo = dot(weighted(mixed, count).T, grad_out) * out_scale
        grad_mixed = (dot(grad_out, out_w.T) * out_scale).astype(BF)
        grad_mixed_c = weighted(grad_mixed, count)
        grad_values = jnp.concatenate(
            [dot(probs[h].T, grad_mixed_c[:, h * HEAD : (h + 1) * HEAD]) for h in range(heads)], axis=1
        ).astype(BF)
        grad_wv = dot(normed.T, weighted(grad_values, count)) * in_scale
        value_w, value_mom, value_sec = adam_update(value_w, peer_v, value_mom, value_sec, grad_wv)
        out_w, out_mom, out_sec = adam_update(out_w, peer_o, out_mom, out_sec, grad_wo)
    return (value_w, out_w, jnp.stack(losses, axis=0))


def on_device(step_index, *rest):
    nbits = lax.axis_size("blk").bit_length() - 1
    return lax.switch(step_index[0] % nbits, [functools.partial(body, e) for e in range(nbits)], *rest)


def solution(mesh):
    in_specs = (
        P(),
        P("blk", None, None),
        P("blk", None),
        P("blk", None),
        P(),
        P(None, "tp"),
        P(None, "tp"),
        P("blk", "tp"),
        P(("blk", "tp"), None),
        P("blk", "tp"),
        P("blk", "tp"),
        P(("blk", "tp"), None),
        P(("blk", "tp"), None),
    )
    out_specs = (P("blk", "tp"), P(("blk", "tp"), None), P("blk", "tp"))
    return jax.shard_map(on_device, mesh=mesh, in_specs=in_specs, out_specs=out_specs, check_vma=False)
```

```python
import functools

import jax
import jax.numpy as jnp
from jax import lax
from jax.experimental import pallas as pl
from jax.experimental.pallas import tpu as pltpu
from jax.sharding import PartitionSpec as P

HEAD = 128
CHUNKS = 4

beta_one = 0.9
beta_two = 0.95
learn_rate = 0.05
decay_rate = 0.1
epsilon = 1e-08

BF = jnp.bfloat16
F32 = jnp.float32
MESH = pl.DeviceIdType.MESH
NT = (((1,), (1,)), ((), ()))
TN = (((0,), (0,)), ((), ()))


def dot(a, b):
    return jnp.dot(a, b, preferred_element_type=F32)


def dotg(a, b, dims):
    return lax.dot_general(a, b, dims, preferred_element_type=F32)


def window(i, n):
    return pl.ds(pl.multiple_of(i * n, n), n)


def kernel(
    start,
    n_blk,
    groups,
    ids_ref,
    gain_ref,
    noisy,
    clean,
    q,
    k,
    v,
    o,
    vm,
    vv,
    om,
    ov,
    v_out,
    o_out,
    loss_out,
    xb,
    cb,
    qb,
    kb,
    v0,
    o0,
    v1,
    o1,
    v2,
    o2,
    vmb,
    vvb,
    omb,
    ovb,
    pv,
    po,
    nb,
    nt,
    sc,
    pb,
    mx,
    mt,
    cc,
    gm,
    gw,
    gbv,
    gbo,
    lacc,
    sb,
    rb,
    go,
    lb,
    load_sem,
    out_sem,
    ex_send,
    ex_recv,
    rs_send,
    rs_recv,
    ag_send,
    ag_recv,
    ls_send,
    ls_recv,
):
    blk = lax.axis_index("blk")
    rank = lax.axis_index("tp")
    nbits = n_blk.bit_length() - 1
    rows, dim = xb.shape
    inner = qb.shape[1]
    heads = inner // HEAD
    width = dim // CHUNKS
    own = rows // groups
    in_scale = dim ** (-0.5)
    out_scale = (inner * groups) ** (-0.5)
    score_scale = HEAD ** (-0.5)
    to, behind = [], []
    for s in range(2):
        distance = 1 << ((start + s) % nbits)
        to.append((lax.rem(blk + distance, n_blk), rank))
        behind.append((lax.rem(blk + n_blk - distance, n_blk), rank))
    mine = window(rank, own)

    def partner(j):
        return lax.rem(rank + j, groups)

    loads = {}
    for i, (name, src, dst) in enumerate(
        (
            ("x", noisy, xb),
            ("q", q, qb),
            ("k", k, kb),
            ("v", v, v0),
            ("o", o, o0),
            ("c", clean.at[mine], cb),
            ("vm", vm, vmb),
            ("vv", vv, vvb),
            ("om", om, omb),
            ("ov", ov, ovb),
        )
    ):
        loads[name] = pltpu.make_async_copy(src, dst, load_sem.at[i])
        loads[name].start()

    barrier = pltpu.get_barrier_semaphore()
    greeted = [to[0], to[1], behind[0], behind[1]] + [(blk, partner(j)) for j in range(1, groups)]
    for device in greeted:
        pl.semaphore_signal(barrier, inc=1, device_id=device, device_id_type=MESH)
    pl.semaphore_wait(barrier, len(greeted))

    def exchange_v(s):
        return pltpu.make_async_remote_copy(
            src_ref=v if s == 0 else v1,
            dst_ref=pv.at[s],
            send_sem=ex_send.at[s, CHUNKS],
            recv_sem=ex_recv.at[s, CHUNKS],
            device_id=to[s],
            device_id_type=MESH,
        )

    def exchange_o0():
        return pltpu.make_async_remote_copy(
            src_ref=o,
            dst_ref=po.at[0],
            send_sem=ex_send.at[0, 0],
            recv_sem=ex_recv.at[0, 0],
            device_id=to[0],
            device_id_type=MESH,
        )

    def exchange_o1(c):
        cols = window(c, width)
        return pltpu.make_async_remote_copy(
            src_ref=o1.at[:, cols],
            dst_ref=po.at[1, :, cols],
            send_sem=ex_send.at[1, c],
            recv_sem=ex_recv.at[1, c],
            device_id=to[1],
            device_id_type=MESH,
        )

    exchange_v(0).start()
    exchange_o0().start()

    def rs_copy(s, c, j):
        t = partner(j)
        return pltpu.make_async_remote_copy(
            src_ref=sb.at[s, c, window(t, own)],
            dst_ref=rb.at[s, c, j],
            send_sem=rs_send.at[s, c, j],
            recv_sem=rs_recv.at[s, c, j],
            device_id=(blk, t),
            device_id_type=MESH,
        )

    def ag_copy(s, c, j):
        return pltpu.make_async_remote_copy(
            src_ref=go.at[s, c, mine],
            dst_ref=go.at[s, c, mine],
            send_sem=ag_send.at[s, c, j],
            recv_sem=ag_recv.at[s, c, j],
            device_id=(blk, partner(j)),
            device_id_type=MESH,
        )

    def ls_copy(s, j):
        return pltpu.make_async_remote_copy(
            src_ref=lb.at[s, mine],
            dst_ref=lb.at[s, mine],
            send_sem=ls_send.at[s, j],
            recv_sem=ls_recv.at[s, j],
            device_id=(blk, partner(j)),
            device_id_type=MESH,
        )

    def each(n, fn):
        def step(i, carry):
            fn(i)
            return carry

        lax.fori_loop(0, n, step, 0)

    def present(s):
        return lax.broadcasted_iota(jnp.int32, (rows, ids_ref.shape[1]), 0) == ids_ref[s : s + 1, :]

    def weighted(x, s):
        return (x.astype(F32) * cc[s]).astype(BF)

    loads["x"].wait()
    tile = 16

    def norm_tile(i):
        at = window(i, tile)
        wide = xb[at, :].astype(F32)
        mean_sq = jnp.mean(wide * wide, axis=-1, keepdims=True)
        nb[at, :] = (wide * lax.rsqrt(mean_sq + 1e-05) * gain_ref[...].astype(F32)).astype(BF)

    each(rows // tile, norm_tile)
    loads["q"].wait()
    queries = (dot(nb[...], qb[...]) * in_scale).astype(BF)
    loads["k"].wait()
    keys = (dot(nb[...], kb[...]) * in_scale).astype(BF)
    for h in range(heads):
        at = slice(h * HEAD, (h + 1) * HEAD)
        sc[h] = dotg(queries[:, at], keys[:, at], NT) * score_scale

    def probabilities(s):
        hot = present(s).astype(F32)
        column = jnp.sum(hot, axis=1, keepdims=True)
        cc[s] = jnp.broadcast_to(column, (rows, inner))
        line = dotg(jnp.ones((8, hot.shape[1]), BF), hot.astype(BF), NT)[0:1, :]
        for h in range(heads):
            score = jnp.where(line > 0.0, sc[h], -jnp.inf)
            expo = jnp.exp(score - jnp.max(score, axis=-1, keepdims=True))
            total = jnp.sum(expo * line, axis=-1, keepdims=True)
            pb[s, h] = (expo / total).astype(BF)

    def mix(s, weight):
        values = weighted((dot(nb[...], weight[...]) * in_scale).astype(BF), s)
        for h in range(heads):
            at = slice(h * HEAD, (h + 1) * HEAD)
            mx[s, :, at] = dot(pb[s, h], values[:, at]).astype(BF)

    def mix_turned(s):
        mt[s] = (mx[s].astype(F32) * cc[s]).T.astype(BF)

    def partial_chunk(s, weight, c):
        part = dot(mx[s], weight[:, window(c, width)]) * out_scale
        sb[s, c] = part.astype(BF)
        each(groups - 1, lambda j: rs_copy(s, c, j + 1).start())

    def reduce_chunk(s, c):
        cols = window(c, width)
        each(groups - 1, lambda j: rs_copy(s, c, j + 1).wait_recv())
        summed = sb[s, c, mine].astype(F32)
        for j in range(1, groups):
            summed = summed + rb[s, c, j].astype(F32)
        error = xb[mine, cols].astype(F32) + summed - cb[:, cols].astype(F32)
        lacc[...] = lacc[...] + jnp.sum(error * error, axis=-1, keepdims=True)
        go[s, c, mine] = error.astype(BF)
        each(groups - 1, lambda j: ag_copy(s, c, j + 1).start())

    def error_parts(s):
        lacc[...] = jnp.zeros_like(lacc)
        each(CHUNKS, functools.partial(reduce_chunk, s))
        lb[s, mine] = lacc[...] * (1.0 / dim)
        each(groups - 1, lambda j: ls_copy(s, j + 1).start())

    def grad_mixed_chunk(s, weight, c):
        each(groups - 1, lambda j: ag_copy(s, c, j + 1).wait_recv())
        gm[...] = gm[...] + dotg(go[s, c], weight[:, window(c, width)], NT)

    def grad_values(s, weight):
        gm[...] = jnp.zeros_like(gm)
        each(CHUNKS, functools.partial(grad_mixed_chunk, s, weight))
        grad_mixed = weighted((gm[...] * out_scale).astype(BF), s)
        for h in range(heads):
            at = slice(h * HEAD, (h + 1) * HEAD)
            gw[:, at] = weighted_half(dotg(pb[s, h], grad_mixed[:, at], TN).astype(BF), s)

    def weighted_half(x, s):
        return (x.astype(F32) * cc[s, :, :HEAD]).astype(BF)

    def adam(grad, moment, second, old, peer, new, keep, at):
        g = grad
        first = beta_one * moment[at].astype(F32) + (1.0 - beta_one) * g
        square = beta_two * second[at].astype(F32) + (1.0 - beta_two) * g * g
        middle = 0.5 * (old[at].astype(F32) + peer[at].astype(F32))
        updated = middle - learn_rate * (first / (jnp.sqrt(square) + epsilon) + decay_rate * middle)
        new[at] = updated.astype(BF)
        if keep:
            moment[at] = first.astype(BF)
            second[at] = square.astype(BF)

    def update_v_chunk(s, old, new, i):
        step = dim // CHUNKS
        gbv[...] = dot(nt[window(i, step), :], gw[...]) * in_scale

        def one(t):
            adam(gbv[window(t, 32), :], vmb, vvb, old, pv.at[s], new, s == 0, (pl.ds(pl.multiple_of(i * step + t * 32, 32), 32), slice(None)))

        each(step // 32, one)

    def update_o_chunk(s, old, new, c):
        gbo[...] = dot(mt[s], go[s, c]) * out_scale

        def one(t):
            adam(gbo[window(t, tile), :], omb, ovb, old, po.at[s], new, s == 0, (window(t, tile), window(c, width)))

        each(inner // tile, one)

    probabilities(0)
    loads["v"].wait()
    mix(0, v0)
    loads["o"].wait()
    each(CHUNKS, functools.partial(partial_chunk, 0, o0))
    probabilities(1)
    mix_turned(0)

    def turn(i):
        nt[window(i, rows), :] = nb[:, window(i, rows)].astype(F32).T.astype(BF)

    each(dim // rows, turn)
    loads["c"].wait()
    error_parts(0)
    grad_values(0, o0)
    for name in ("vm", "vv", "om", "ov"):
        loads[name].wait()
    exchange_v(0).wait_recv()
    each(CHUNKS, functools.partial(update_v_chunk, 0, v0, v1))
    exchange_v(1).start()

    mix(1, v1)
    exchange_o0().wait_recv()

    def next_chunk(c):
        update_o_chunk(0, o0, o1, c)
        exchange_o1(c).start()
        partial_chunk(1, o1, c)

    each(CHUNKS, next_chunk)
    mix_turned(1)
    error_parts(1)
    grad_values(1, o1)
    exchange_v(1).wait_recv()

    def out_v(i):
        at = window(i, dim // CHUNKS)
        return pltpu.make_async_copy(v2.at[at, :], v_out.at[at, :], out_sem.at[0, i])

    def out_o(c):
        cols = window(c, width)
        return pltpu.make_async_copy(o2.at[:, cols], o_out.at[:, cols], out_sem.at[1, c])

    def last_v(i):
        update_v_chunk(1, v1, v2, i)
        out_v(i).start()

    each(CHUNKS, last_v)

    def last_o(c):
        exchange_o1(c).wait_recv()
        update_o_chunk(1, o1, o2, c)
        out_o(c).start()

    each(CHUNKS, last_o)

    share = loss_out.shape[1]
    for s in range(2):
        each(groups - 1, lambda j: ls_copy(s, j + 1).wait_recv())
        picked = jnp.sum(jnp.where(present(s), lb[s][:, 0:1], 0.0), axis=0, keepdims=True)
        chosen = jnp.zeros((1, share), F32)
        for g in range(groups):
            chosen = jnp.where(rank == g, picked[:, g * share : (g + 1) * share], chosen)
        loss_out[s : s + 1, :] = chosen

    exchange_v(0).wait_send()
    exchange_o0().wait_send()
    exchange_v(1).wait_send()
    each(CHUNKS, lambda c: exchange_o1(c).wait_send())
    for s in range(2):

        def sent(c):
            each(groups - 1, lambda j: rs_copy(s, c, j + 1).wait_send())
            each(groups - 1, lambda j: ag_copy(s, c, j + 1).wait_send())

        each(CHUNKS, sent)
        each(groups - 1, lambda j: ls_copy(s, j + 1).wait_send())
    each(CHUNKS, lambda i: out_v(i).wait())
    each(CHUNKS, lambda c: out_o(c).wait())


def train(start, ids, gain, noisy, clean, q, k, v, o, vm, vv, om, ov):
    n_blk, groups = lax.axis_size("blk"), lax.axis_size("tp")
    rows, dim = noisy.shape
    inner = q.shape[1]
    width = dim // CHUNKS
    own = rows // groups
    vec = pl.BlockSpec(memory_space=pltpu.VMEM)
    hbm = pl.BlockSpec(memory_space=pl.ANY)
    V = pltpu.VMEM
    dma = pltpu.SemaphoreType.DMA
    tall, flat = V((dim, inner), BF), V((inner, dim), BF)
    return pl.pallas_call(
        functools.partial(kernel, start, n_blk, groups),
        out_shape=(
            jax.ShapeDtypeStruct(v.shape, BF),
            jax.ShapeDtypeStruct(o.shape, BF),
            jax.ShapeDtypeStruct((2, ids.shape[1] // groups), F32),
        ),
        in_specs=[vec, vec] + [hbm] * 10,
        out_specs=(hbm, hbm, vec),
        scratch_shapes=[
            V((rows, dim), BF),
            V((own, dim), BF),
            tall,
            tall,
            tall,
            flat,
            tall,
            flat,
            tall,
            flat,
            tall,
            tall,
            flat,
            flat,
            V((2, dim, inner), BF),
            V((2, inner, dim), BF),
            V((rows, dim), BF),
            V((dim, rows), BF),
            V((inner // HEAD, rows, rows), F32),
            V((2, inner // HEAD, rows, rows), BF),
            V((2, rows, inner), BF),
            V((2, inner, rows), BF),
            V((2, rows, inner), F32),
            V((rows, inner), F32),
            V((rows, inner), BF),
            V((dim // CHUNKS, inner), F32),
            V((inner, width), F32),
            V((own, 128), F32),
            V((2, CHUNKS, rows, width), BF),
            V((2, CHUNKS, groups, own, width), BF),
            V((2, CHUNKS, rows, width), BF),
            V((2, rows, 128), F32),
            dma((10,)),
            dma((2, CHUNKS)),
            dma((2, CHUNKS + 1)),
            dma((2, CHUNKS + 1)),
            dma((2, CHUNKS, groups)),
            dma((2, CHUNKS, groups)),
            dma((2, CHUNKS, groups)),
            dma((2, CHUNKS, groups)),
            dma((2, groups)),
            dma((2, groups)),
        ],
        compiler_params=pltpu.CompilerParams(
            collective_id=start, has_side_effects=True, vmem_limit_bytes=56 << 20
        ),
        cost_estimate=pl.CostEstimate(flops=3_200_000_000, bytes_accessed=12 << 20, transcendentals=0),
        name=f"train_{start}",
    )(ids, gain, noisy, clean, q, k, v, o, vm, vv, om, ov)


def on_device(step_index, patch_ids, noisy_pool, clean_pool, norm_gain, q_weight, k_weight, value_weight, out_weight, value_m, value_v, out_m, out_v):
    nbits = lax.axis_size("blk").bit_length() - 1
    return lax.switch(
        step_index[0] % nbits,
        [functools.partial(train, e) for e in range(nbits)],
        patch_ids[0],
        norm_gain[None, :],
        noisy_pool,
        clean_pool,
        q_weight,
        k_weight,
        value_weight,
        out_weight,
        value_m,
        value_v,
        out_m,
        out_v,
    )


def solution(mesh):
    in_specs = (
        P(),
        P("blk", None, None),
        P("blk", None),
        P("blk", None),
        P(),
        P(None, "tp"),
        P(None, "tp"),
        P("blk", "tp"),
        P(("blk", "tp"), None),
        P("blk", "tp"),
        P("blk", "tp"),
        P(("blk", "tp"), None),
        P(("blk", "tp"), None),
    )
    out_specs = (P("blk", "tp"), P(("blk", "tp"), None), P("blk", "tp"))
    return jax.shard_map(on_device, mesh=mesh, in_specs=in_specs, out_specs=out_specs, check_vma=False)
```

```python
import functools

import jax
import jax.numpy as jnp
from jax import lax
from jax.experimental import pallas as pl
from jax.experimental.pallas import tpu as pltpu
from jax.sharding import PartitionSpec as P

HEAD = 128
CHUNKS = 4

beta_one = 0.9
beta_two = 0.95
learn_rate = 0.05
decay_rate = 0.1
epsilon = 1e-08

BF = jnp.bfloat16
F32 = jnp.float32
MESH = pl.DeviceIdType.MESH
NT = (((1,), (1,)), ((), ()))
TN = (((0,), (0,)), ((), ()))


def dot(a, b):
    return jnp.dot(a, b, preferred_element_type=F32)


def dotg(a, b, dims):
    return lax.dot_general(a, b, dims, preferred_element_type=F32)


def window(i, n):
    return pl.ds(pl.multiple_of(i * n, n), n)


def kernel(
    start,
    n_blk,
    groups,
    ids_ref,
    gain_ref,
    noisy,
    clean,
    q,
    k,
    v,
    o,
    vm,
    vv,
    om,
    ov,
    v_out,
    o_out,
    loss_out,
    xb,
    cb,
    qb,
    kb,
    v0,
    o0,
    v1,
    o1,
    v2,
    o2,
    vmb,
    vvb,
    omb,
    ovb,
    pv,
    po,
    nb,
    nt,
    sc,
    pb,
    mx,
    mt,
    cc,
    gm,
    gw,
    gbv,
    gbo,
    lacc,
    sb,
    ry,
    xs,
    xr,
    held,
    go,
    lb,
    load_sem,
    out_sem,
    ex_send,
    ex_recv,
    ry_send,
    ry_recv,
    rx_send,
    rx_recv,
    gx_send,
    gx_recv,
    gy_send,
    gy_recv,
    ls_send,
    ls_recv,
    grant_sem,
):
    blk = lax.axis_index("blk")
    rank = lax.axis_index("tp")
    nbits = n_blk.bit_length() - 1
    rows, dim = xb.shape
    inner = qb.shape[1]
    heads = inner // HEAD
    width = dim // CHUNKS
    own = rows // groups
    in_scale = dim ** (-0.5)
    out_scale = (inner * groups) ** (-0.5)
    score_scale = HEAD ** (-0.5)
    to, behind = [], []
    for s in range(2):
        distance = 1 << ((start + s) % nbits)
        to.append((lax.rem(blk + distance, n_blk), rank))
        behind.append((lax.rem(blk + n_blk - distance, n_blk), rank))
    mine = window(rank, own)

    def partner(j):
        return lax.rem(rank + j, groups)

    loads = {}
    for i, (name, src, dst) in enumerate(
        (
            ("x", noisy, xb),
            ("q", q, qb),
            ("k", k, kb),
            ("v", v, v0),
            ("o", o, o0),
            ("c", clean.at[mine], cb),
            ("vm", vm, vmb),
            ("vv", vv, vvb),
            ("om", om, omb),
            ("ov", ov, ovb),
        )
    ):
        loads[name] = pltpu.make_async_copy(src, dst, load_sem.at[i])
        loads[name].start()

    barrier = pltpu.get_barrier_semaphore()
    greeted = [to[0], to[1], behind[0], behind[1]] + [(blk, partner(j)) for j in range(1, groups)]
    for device in greeted:
        pl.semaphore_signal(barrier, inc=1, device_id=device, device_id_type=MESH)
    pl.semaphore_wait(barrier, len(greeted))

    def exchange_v(s):
        return pltpu.make_async_remote_copy(
            src_ref=v if s == 0 else v1,
            dst_ref=pv.at[s],
            send_sem=ex_send.at[s, 0],
            recv_sem=ex_recv.at[s, 0],
            device_id=to[s],
            device_id_type=MESH,
        )

    def exchange_o(s):
        return pltpu.make_async_remote_copy(
            src_ref=o if s == 0 else o1,
            dst_ref=po.at[s],
            send_sem=ex_send.at[s, 1],
            recv_sem=ex_recv.at[s, 1],
            device_id=to[s],
            device_id_type=MESH,
        )

    far = 1 << start % nbits == n_blk // 4
    granted = [1 << (start + s) % nbits not in (4, 8) for s in range(2)]

    def send_when_granted(s):
        pl.semaphore_signal(grant_sem.at[s], inc=1, device_id=behind[s], device_id_type=MESH)
        pl.semaphore_wait(grant_sem.at[s], 1)
        exchange_o(s).start()

    exchange_v(0).start()
    if not far and not granted[0]:
        exchange_o(0).start()

    along = groups // 2
    y, x = rank // 2, lax.rem(rank, 2)
    across = (blk, 2 * y + 1 - x)
    column = window(y, 2 * own)

    def ry_copy(s, c, j):
        t = lax.rem(y + j, along)
        return pltpu.make_async_remote_copy(
            src_ref=sb.at[s, c, window(t, 2 * own)],
            dst_ref=ry.at[s, c, j],
            send_sem=ry_send.at[s, c, j],
            recv_sem=ry_recv.at[s, c, j],
            device_id=(blk, 2 * t + x),
            device_id_type=MESH,
        )

    def rx_copy(s, c):
        return pltpu.make_async_remote_copy(
            src_ref=xs.at[s, c],
            dst_ref=xr.at[s, c],
            send_sem=rx_send.at[s, c],
            recv_sem=rx_recv.at[s, c],
            device_id=across,
            device_id_type=MESH,
        )

    def gx_copy(s, c):
        return pltpu.make_async_remote_copy(
            src_ref=go.at[s, c, mine],
            dst_ref=go.at[s, c, mine],
            send_sem=gx_send.at[s, c],
            recv_sem=gx_recv.at[s, c],
            device_id=across,
            device_id_type=MESH,
        )

    def gy_copy(s, c, j):
        t = lax.rem(y + j, along)
        return pltpu.make_async_remote_copy(
            src_ref=go.at[s, c, column],
            dst_ref=go.at[s, c, column],
            send_sem=gy_send.at[s, c, j],
            recv_sem=gy_recv.at[s, c, j],
            device_id=(blk, 2 * t + x),
            device_id_type=MESH,
        )

    def ls_copy(s, j):
        return pltpu.make_async_remote_copy(
            src_ref=lb.at[s, mine],
            dst_ref=lb.at[s, mine],
            send_sem=ls_send.at[s, j],
            recv_sem=ls_recv.at[s, j],
            device_id=(blk, partner(j)),
            device_id_type=MESH,
        )

    def each(n, fn, unroll=1):
        def step(i, carry):
            fn(i)
            return carry

        lax.fori_loop(0, n, step, 0, unroll=unroll)

    def present(s):
        return lax.broadcasted_iota(jnp.int32, (rows, ids_ref.shape[1]), 0) == ids_ref[s : s + 1, :]

    def weighted(x, s):
        return (x.astype(F32) * cc[s]).astype(BF)

    loads["x"].wait()
    tile = 16

    def norm_tile(i):
        at = window(i, tile)
        wide = xb[at, :].astype(F32)
        mean_sq = jnp.mean(wide * wide, axis=-1, keepdims=True)
        nb[at, :] = (wide * lax.rsqrt(mean_sq + 1e-05) * gain_ref[...].astype(F32)).astype(BF)

    each(rows // tile, norm_tile)
    loads["q"].wait()
    queries = (dot(nb[...], qb[...]) * in_scale).astype(BF)
    loads["k"].wait()
    keys = (dot(nb[...], kb[...]) * in_scale).astype(BF)
    for h in range(heads):
        at = slice(h * HEAD, (h + 1) * HEAD)
        sc[h] = dotg(queries[:, at], keys[:, at], NT) * score_scale

    def probabilities(s):
        hot = present(s).astype(F32)
        column = jnp.sum(hot, axis=1, keepdims=True)
        cc[s] = jnp.broadcast_to(column, (rows, inner))
        line = dotg(jnp.ones((8, hot.shape[1]), BF), hot.astype(BF), NT)[0:1, :]
        for h in range(heads):
            score = jnp.where(line > 0.0, sc[h], -jnp.inf)
            expo = jnp.exp(score - jnp.max(score, axis=-1, keepdims=True))
            total = jnp.sum(expo * line, axis=-1, keepdims=True)
            pb[s, h] = (expo / total).astype(BF)

    def mix(s, weight):
        values = weighted((dot(nb[...], weight[...]) * in_scale).astype(BF), s)
        for h in range(heads):
            at = slice(h * HEAD, (h + 1) * HEAD)
            mx[s, :, at] = dot(pb[s, h], values[:, at]).astype(BF)

    def mix_turned(s):
        mt[s] = (mx[s].astype(F32) * cc[s]).T.astype(BF)

    def partial_chunk(s, weight, c):
        part = dot(mx[s], weight[:, window(c, width)]) * out_scale
        sb[s, c] = part.astype(BF)
        each(along - 1, lambda j: ry_copy(s, c, j + 1).start())

    def sum_along(s, c):
        each(along - 1, lambda j: ry_copy(s, c, j + 1).wait_recv())

        def total(half):
            summed = sb[s, c, pl.ds(pl.multiple_of(y * 2 * own + half * own, own), own)].astype(F32)
            for j in range(1, along):
                summed = summed + ry[s, c, j, window(half, own)].astype(F32)
            return summed

        xs[s, c] = total(1 - x).astype(BF)
        rx_copy(s, c).start()
        held[c] = total(x)

    def finish_error(s, c):
        cols = window(c, width)
        rx_copy(s, c).wait_recv()
        summed = held[c] + xr[s, c].astype(F32)
        error = xb[mine, cols].astype(F32) + summed - cb[:, cols].astype(F32)
        go[s, c, mine] = error.astype(BF)
        gx_copy(s, c).start()
        lacc[...] = lacc[...] + jnp.sum(error * error, axis=-1, keepdims=True)

    def pass_on(s, c):
        gx_copy(s, c).wait_recv()
        each(along - 1, lambda j: gy_copy(s, c, j + 1).start())

    def error_parts(s):
        lacc[...] = jnp.zeros_like(lacc)
        sum_along(s, 0)
        sum_along(s, 1)
        finish_error(s, 0)

        def middle(i):
            sum_along(s, i + 2)
            finish_error(s, i + 1)
            pass_on(s, i)

        each(CHUNKS - 2, middle)
        finish_error(s, CHUNKS - 1)
        pass_on(s, CHUNKS - 2)
        pass_on(s, CHUNKS - 1)
        lb[s, mine] = lacc[...] * (1.0 / dim)
        each(groups - 1, lambda j: ls_copy(s, j + 1).start())

    def grad_mixed_chunk(s, weight, c):
        each(along - 1, lambda j: gy_copy(s, c, j + 1).wait_recv())
        gm[...] = gm[...] + dotg(go[s, c], weight[:, window(c, width)], NT)

    def grad_values(s, weight):
        gm[...] = jnp.zeros_like(gm)
        each(CHUNKS, functools.partial(grad_mixed_chunk, s, weight))
        grad_mixed = weighted((gm[...] * out_scale).astype(BF), s)
        for h in range(heads):
            at = slice(h * HEAD, (h + 1) * HEAD)
            gw[:, at] = weighted_half(dotg(pb[s, h], grad_mixed[:, at], TN).astype(BF), s)

    def weighted_half(x, s):
        return (x.astype(F32) * cc[s, :, :HEAD]).astype(BF)

    def adam(grad, moment, second, old, peer, new, keep, at):
        g = grad
        first = beta_one * moment[at].astype(F32) + (1.0 - beta_one) * g
        square = beta_two * second[at].astype(F32) + (1.0 - beta_two) * g * g
        middle = 0.5 * (old[at].astype(F32) + peer[at].astype(F32))
        updated = middle - learn_rate * (first / (jnp.sqrt(square) + epsilon) + decay_rate * middle)
        new[at] = updated.astype(BF)
        if keep:
            moment[at] = first.astype(BF)
            second[at] = square.astype(BF)

    def update_v_chunk(s, old, new, i):
        step = dim // CHUNKS
        gbv[...] = dot(nt[window(i, step), :], gw[...]) * in_scale

        def one(t):
            adam(gbv[window(t, 32), :], vmb, vvb, old, pv.at[s], new, s == 0, (pl.ds(pl.multiple_of(i * step + t * 32, 32), 32), slice(None)))

        each(step // 32, one, 2)

    def update_o_chunk(s, old, new, c):
        gbo[...] = dot(mt[s], go[s, c]) * out_scale

        def one(t):
            adam(gbo[window(t, tile), :], omb, ovb, old, po.at[s], new, s == 0, (window(t, tile), window(c, width)))

        each(inner // tile, one, 2)

    probabilities(0)
    loads["v"].wait()
    mix(0, v0)
    loads["o"].wait()
    each(CHUNKS, functools.partial(partial_chunk, 0, o0))
    probabilities(1)
    mix_turned(0)

    def turn(i):
        nt[window(i, rows), :] = nb[:, window(i, rows)].astype(F32).T.astype(BF)

    each(dim // rows, turn)
    loads["c"].wait()
    error_parts(0)
    if granted[0]:
        send_when_granted(0)
    grad_values(0, o0)
    if far:
        exchange_v(0).wait_send()
        exchange_o(0).start()
    for name in ("vm", "vv", "om", "ov"):
        loads[name].wait()
    exchange_v(0).wait_recv()
    each(CHUNKS, functools.partial(update_v_chunk, 0, v0, v1))
    exchange_v(1).start()

    mix(1, v1)
    exchange_o(0).wait_recv()

    def next_chunk(c):
        update_o_chunk(0, o0, o1, c)
        partial_chunk(1, o1, c)

    each(CHUNKS, next_chunk)
    if not granted[1]:
        exchange_o(1).start()
    mix_turned(1)
    error_parts(1)
    if granted[1]:
        send_when_granted(1)
    grad_values(1, o1)
    exchange_v(1).wait_recv()

    def out_v(i):
        at = window(i, dim // CHUNKS)
        return pltpu.make_async_copy(v2.at[at, :], v_out.at[at, :], out_sem.at[0, i])

    def out_o(c):
        cols = window(c, width)
        return pltpu.make_async_copy(o2.at[:, cols], o_out.at[:, cols], out_sem.at[1, c])

    def last_v(i):
        update_v_chunk(1, v1, v2, i)
        out_v(i).start()

    each(CHUNKS, last_v)

    exchange_o(1).wait_recv()

    def last_o(c):
        update_o_chunk(1, o1, o2, c)
        out_o(c).start()

    each(CHUNKS, last_o)

    share = loss_out.shape[1]
    for s in range(2):
        each(groups - 1, lambda j: ls_copy(s, j + 1).wait_recv())
        picked = jnp.sum(jnp.where(present(s), lb[s][:, 0:1], 0.0), axis=0, keepdims=True)
        chosen = jnp.zeros((1, share), F32)
        for g in range(groups):
            chosen = jnp.where(rank == g, picked[:, g * share : (g + 1) * share], chosen)
        loss_out[s : s + 1, :] = chosen

    for s in range(2):
        exchange_o(s).wait_send()
        if s == 1 or not far:
            exchange_v(s).wait_send()

        def sent(c):
            each(along - 1, lambda j: ry_copy(s, c, j + 1).wait_send())
            rx_copy(s, c).wait_send()
            gx_copy(s, c).wait_send()
            each(along - 1, lambda j: gy_copy(s, c, j + 1).wait_send())

        each(CHUNKS, sent)
        each(groups - 1, lambda j: ls_copy(s, j + 1).wait_send())
    each(CHUNKS, lambda i: out_v(i).wait())
    each(CHUNKS, lambda c: out_o(c).wait())


def train(start, ids, gain, noisy, clean, q, k, v, o, vm, vv, om, ov):
    n_blk, groups = lax.axis_size("blk"), lax.axis_size("tp")
    rows, dim = noisy.shape
    inner = q.shape[1]
    width = dim // CHUNKS
    own = rows // groups
    vec = pl.BlockSpec(memory_space=pltpu.VMEM)
    hbm = pl.BlockSpec(memory_space=pl.ANY)
    V = pltpu.VMEM
    dma = pltpu.SemaphoreType.DMA
    tall, flat = V((dim, inner), BF), V((inner, dim), BF)
    return pl.pallas_call(
        functools.partial(kernel, start, n_blk, groups),
        out_shape=(
            jax.ShapeDtypeStruct(v.shape, BF),
            jax.ShapeDtypeStruct(o.shape, BF),
            jax.ShapeDtypeStruct((2, ids.shape[1] // groups), F32),
        ),
        in_specs=[vec, vec] + [hbm] * 10,
        out_specs=(hbm, hbm, vec),
        scratch_shapes=[
            V((rows, dim), BF),
            V((own, dim), BF),
            tall,
            tall,
            tall,
            flat,
            tall,
            flat,
            tall,
            flat,
            tall,
            tall,
            flat,
            flat,
            V((2, dim, inner), BF),
            V((2, inner, dim), BF),
            V((rows, dim), BF),
            V((dim, rows), BF),
            V((inner // HEAD, rows, rows), F32),
            V((2, inner // HEAD, rows, rows), BF),
            V((2, rows, inner), BF),
            V((2, inner, rows), BF),
            V((2, rows, inner), F32),
            V((rows, inner), F32),
            V((rows, inner), BF),
            V((dim // CHUNKS, inner), F32),
            V((inner, width), F32),
            V((own, 128), F32),
            V((2, CHUNKS, rows, width), BF),
            V((2, CHUNKS, groups // 2, 2 * own, width), BF),
            V((2, CHUNKS, own, width), BF),
            V((2, CHUNKS, own, width), BF),
            V((CHUNKS, own, width), F32),
            V((2, CHUNKS, rows, width), BF),
            V((2, rows, 128), F32),
            dma((10,)),
            dma((2, CHUNKS)),
            dma((2, 2)),
            dma((2, 2)),
            dma((2, CHUNKS, groups // 2)),
            dma((2, CHUNKS, groups // 2)),
            dma((2, CHUNKS)),
            dma((2, CHUNKS)),
            dma((2, CHUNKS)),
            dma((2, CHUNKS)),
            dma((2, CHUNKS, groups // 2)),
            dma((2, CHUNKS, groups // 2)),
            dma((2, groups)),
            dma((2, groups)),
            pltpu.SemaphoreType.REGULAR((2,)),
        ],
        compiler_params=pltpu.CompilerParams(
            collective_id=start, has_side_effects=True, vmem_limit_bytes=56 << 20
        ),
        cost_estimate=pl.CostEstimate(flops=3_200_000_000, bytes_accessed=12 << 20, transcendentals=0),
        name=f"train_{start}",
    )(ids, gain, noisy, clean, q, k, v, o, vm, vv, om, ov)


def on_device(step_index, patch_ids, noisy_pool, clean_pool, norm_gain, q_weight, k_weight, value_weight, out_weight, value_m, value_v, out_m, out_v):
    nbits = lax.axis_size("blk").bit_length() - 1
    return lax.switch(
        step_index[0] % nbits,
        [functools.partial(train, e) for e in range(nbits)],
        patch_ids[0],
        norm_gain[None, :],
        noisy_pool,
        clean_pool,
        q_weight,
        k_weight,
        value_weight,
        out_weight,
        value_m,
        value_v,
        out_m,
        out_v,
    )


def solution(mesh):
    in_specs = (
        P(),
        P("blk", None, None),
        P("blk", None),
        P("blk", None),
        P(),
        P(None, "tp"),
        P(None, "tp"),
        P("blk", "tp"),
        P(("blk", "tp"), None),
        P("blk", "tp"),
        P("blk", "tp"),
        P(("blk", "tp"), None),
        P(("blk", "tp"), None),
    )
    out_specs = (P("blk", "tp"), P(("blk", "tp"), None), P("blk", "tp"))
    return jax.shard_map(on_device, mesh=mesh, in_specs=in_specs, out_specs=out_specs, check_vma=False)
```

```python
import functools

import jax
import jax.numpy as jnp
from jax import lax
from jax.experimental import pallas as pl
from jax.experimental.pallas import tpu as pltpu
from jax.sharding import PartitionSpec as P

HEAD = 128
CHUNKS = 4

beta_one = 0.9
beta_two = 0.95
learn_rate = 0.05
decay_rate = 0.1
epsilon = 1e-08

BF = jnp.bfloat16
F32 = jnp.float32
MESH = pl.DeviceIdType.MESH
NT = (((1,), (1,)), ((), ()))
TN = (((0,), (0,)), ((), ()))


def dot(a, b):
    return jnp.dot(a, b, preferred_element_type=F32)


def dotg(a, b, dims):
    return lax.dot_general(a, b, dims, preferred_element_type=F32)


def window(i, n):
    return pl.ds(pl.multiple_of(i * n, n), n)


def kernel(
    start,
    n_blk,
    groups,
    ids_ref,
    gain_ref,
    noisy,
    clean,
    q,
    k,
    v,
    o,
    vm,
    vv,
    om,
    ov,
    v_out,
    o_out,
    loss_out,
    xb,
    cb,
    qb,
    kb,
    v0,
    o0,
    v1,
    o1,
    v2,
    o2,
    vmb,
    vvb,
    omb,
    ovb,
    pv,
    po,
    nb,
    nt,
    sc,
    pb,
    mx,
    mt,
    cc,
    gm,
    gw,
    gbv,
    gbo,
    lacc,
    sb,
    ry,
    xs,
    xr,
    held,
    go,
    lb,
    load_sem,
    out_sem,
    ex_send,
    ex_recv,
    ry_send,
    ry_recv,
    rx_send,
    rx_recv,
    gx_send,
    gx_recv,
    gy_send,
    gy_recv,
    ls_send,
    ls_recv,
    grant_sem,
    leg_send,
    leg_recv,
    relay_v,
    relay_o,
):
    blk = lax.axis_index("blk")
    rank = lax.axis_index("tp")
    nbits = n_blk.bit_length() - 1
    rows, dim = xb.shape
    inner = qb.shape[1]
    heads = inner // HEAD
    width = dim // CHUNKS
    own = rows // groups
    in_scale = dim ** (-0.5)
    out_scale = (inner * groups) ** (-0.5)
    score_scale = HEAD ** (-0.5)
    to, behind = [], []
    for s in range(2):
        distance = 1 << ((start + s) % nbits)
        to.append((lax.rem(blk + distance, n_blk), rank))
        behind.append((lax.rem(blk + n_blk - distance, n_blk), rank))
    mine = window(rank, own)

    def partner(j):
        return lax.rem(rank + j, groups)

    loads = {}
    for i, (name, src, dst) in enumerate(
        (
            ("x", noisy, xb),
            ("q", q, qb),
            ("k", k, kb),
            ("v", v, v0),
            ("o", o, o0),
            ("c", clean.at[mine], cb),
            ("vm", vm, vmb),
            ("vv", vv, vvb),
            ("om", om, omb),
            ("ov", ov, ovb),
        )
    ):
        loads[name] = pltpu.make_async_copy(src, dst, load_sem.at[i])
        loads[name].start()

    barrier = pltpu.get_barrier_semaphore()
    greeted = [to[0], to[1], behind[0], behind[1]] + [(blk, partner(j)) for j in range(1, groups)]
    split = [1 << (start + s) % nbits == 4 for s in range(2)]
    direct = [dim * 3 // 4 if split[s] else dim for s in range(2)]

    def chips_on(index, n):
        return 16 * (index // 16) + lax.rem(lax.rem(index, 16) + 2 * n, 16)

    served = chips_on(blk, 3)
    relay, goal = (chips_on(blk, 5), rank), (lax.rem(served + 4, n_blk), rank)
    if split[0] or split[1]:
        greeted += [relay, (served, rank), goal, (chips_on(lax.rem(blk + n_blk - 4, n_blk), 5), rank)]
    for device in greeted:
        pl.semaphore_signal(barrier, inc=1, device_id=device, device_id_type=MESH)
    pl.semaphore_wait(barrier, len(greeted))

    def exchange_v(s):
        part = pl.ds(0, direct[s])
        return pltpu.make_async_remote_copy(
            src_ref=(v, v1)[s].at[part, :],
            dst_ref=pv.at[s, part, :],
            send_sem=ex_send.at[s, 0],
            recv_sem=ex_recv.at[s, 0],
            device_id=to[s],
            device_id_type=MESH,
        )

    def exchange_o(s):
        part = pl.ds(0, direct[s])
        return pltpu.make_async_remote_copy(
            src_ref=(o, o1)[s].at[:, part],
            dst_ref=po.at[s, :, part],
            send_sem=ex_send.at[s, 1],
            recv_sem=ex_recv.at[s, 1],
            device_id=to[s],
            device_id_type=MESH,
        )

    def first_leg(s, which):
        part = pl.ds(dim * 3 // 4, dim // 4)
        return pltpu.make_async_remote_copy(
            src_ref=((v, v1)[s].at[part, :], (o, o1)[s].at[:, part])[which],
            dst_ref=(relay_v, relay_o)[which],
            send_sem=leg_send.at[which],
            recv_sem=leg_recv.at[which],
            device_id=relay,
            device_id_type=MESH,
        )

    def second_leg(s, which):
        part = pl.ds(dim * 3 // 4, dim // 4)
        return pltpu.make_async_remote_copy(
            src_ref=(relay_v, relay_o)[which],
            dst_ref=(pv.at[s, part, :], po.at[s, :, part])[which],
            send_sem=leg_send.at[2 + which],
            recv_sem=leg_recv.at[2 + which],
            device_id=goal,
            device_id_type=MESH,
        )

    def send(s, which):
        if split[s]:
            first_leg(s, which).start()
        (exchange_v, exchange_o)[which](s).start()

    def forward(s, which):
        if split[s]:
            first_leg(s, which).wait_recv()
            second_leg(s, which).start()

    def arrived(s, which):
        (exchange_v, exchange_o)[which](s).wait_recv()
        if split[s]:
            second_leg(s, which).wait_recv()

    far = 1 << start % nbits == n_blk // 4
    granted = [1 << (start + s) % nbits not in (4, 8) for s in range(2)]

    def send_when_granted(s):
        pl.semaphore_signal(grant_sem.at[s], inc=1, device_id=behind[s], device_id_type=MESH)
        pl.semaphore_wait(grant_sem.at[s], 1)
        exchange_o(s).start()

    send(0, 0)
    if not far and not granted[0]:
        send(0, 1)

    along = groups // 2
    y, x = rank // 2, lax.rem(rank, 2)
    across = (blk, 2 * y + 1 - x)
    column = window(y, 2 * own)

    def ry_copy(s, c, j):
        t = lax.rem(y + j, along)
        return pltpu.make_async_remote_copy(
            src_ref=sb.at[s, c, window(t, 2 * own)],
            dst_ref=ry.at[s, c, j],
            send_sem=ry_send.at[s, c, j],
            recv_sem=ry_recv.at[s, c, j],
            device_id=(blk, 2 * t + x),
            device_id_type=MESH,
        )

    def rx_copy(s, c):
        return pltpu.make_async_remote_copy(
            src_ref=xs.at[s, c],
            dst_ref=xr.at[s, c],
            send_sem=rx_send.at[s, c],
            recv_sem=rx_recv.at[s, c],
            device_id=across,
            device_id_type=MESH,
        )

    def gx_copy(s, c):
        return pltpu.make_async_remote_copy(
            src_ref=go.at[s, c, mine],
            dst_ref=go.at[s, c, mine],
            send_sem=gx_send.at[s, c],
            recv_sem=gx_recv.at[s, c],
            device_id=across,
            device_id_type=MESH,
        )

    def gy_copy(s, c, j):
        t = lax.rem(y + j, along)
        return pltpu.make_async_remote_copy(
            src_ref=go.at[s, c, column],
            dst_ref=go.at[s, c, column],
            send_sem=gy_send.at[s, c, j],
            recv_sem=gy_recv.at[s, c, j],
            device_id=(blk, 2 * t + x),
            device_id_type=MESH,
        )

    def ls_copy(s, j):
        return pltpu.make_async_remote_copy(
            src_ref=lb.at[s, mine],
            dst_ref=lb.at[s, mine],
            send_sem=ls_send.at[s, j],
            recv_sem=ls_recv.at[s, j],
            device_id=(blk, partner(j)),
            device_id_type=MESH,
        )

    def each(n, fn, unroll=1):
        def step(i, carry):
            fn(i)
            return carry

        lax.fori_loop(0, n, step, 0, unroll=unroll)

    def present(s):
        return lax.broadcasted_iota(jnp.int32, (rows, ids_ref.shape[1]), 0) == ids_ref[s : s + 1, :]

    def weighted(x, s):
        return (x.astype(F32) * cc[s]).astype(BF)

    loads["x"].wait()
    tile = 16

    def norm_tile(i):
        at = window(i, tile)
        wide = xb[at, :].astype(F32)
        mean_sq = jnp.mean(wide * wide, axis=-1, keepdims=True)
        nb[at, :] = (wide * lax.rsqrt(mean_sq + 1e-05) * gain_ref[...].astype(F32)).astype(BF)

    each(rows // tile, norm_tile)
    loads["q"].wait()
    queries = (dot(nb[...], qb[...]) * in_scale).astype(BF)
    loads["k"].wait()
    keys = (dot(nb[...], kb[...]) * in_scale).astype(BF)
    for h in range(heads):
        at = slice(h * HEAD, (h + 1) * HEAD)
        sc[h] = dotg(queries[:, at], keys[:, at], NT) * score_scale

    def probabilities(s):
        hot = present(s).astype(F32)
        column = jnp.sum(hot, axis=1, keepdims=True)
        cc[s] = jnp.broadcast_to(column, (rows, inner))
        line = dotg(jnp.ones((8, hot.shape[1]), BF), hot.astype(BF), NT)[0:1, :]
        for h in range(heads):
            score = jnp.where(line > 0.0, sc[h], -jnp.inf)
            expo = jnp.exp(score - jnp.max(score, axis=-1, keepdims=True))
            total = jnp.sum(expo * line, axis=-1, keepdims=True)
            pb[s, h] = (expo / total).astype(BF)

    def mix(s, weight):
        values = weighted((dot(nb[...], weight[...]) * in_scale).astype(BF), s)
        for h in range(heads):
            at = slice(h * HEAD, (h + 1) * HEAD)
            mx[s, :, at] = dot(pb[s, h], values[:, at]).astype(BF)

    def mix_turned(s):
        mt[s] = (mx[s].astype(F32) * cc[s]).T.astype(BF)

    def partial_chunk(s, weight, c):
        part = dot(mx[s], weight[:, window(c, width)]) * out_scale
        sb[s, c] = part.astype(BF)
        each(along - 1, lambda j: ry_copy(s, c, j + 1).start())

    def sum_along(s, c):
        each(along - 1, lambda j: ry_copy(s, c, j + 1).wait_recv())

        def total(half):
            summed = sb[s, c, pl.ds(pl.multiple_of(y * 2 * own + half * own, own), own)].astype(F32)
            for j in range(1, along):
                summed = summed + ry[s, c, j, window(half, own)].astype(F32)
            return summed

        xs[s, c] = total(1 - x).astype(BF)
        rx_copy(s, c).start()
        held[c] = total(x)

    def finish_error(s, c):
        cols = window(c, width)
        rx_copy(s, c).wait_recv()
        summed = held[c] + xr[s, c].astype(F32)
        error = xb[mine, cols].astype(F32) + summed - cb[:, cols].astype(F32)
        go[s, c, mine] = error.astype(BF)
        gx_copy(s, c).start()
        lacc[...] = lacc[...] + jnp.sum(error * error, axis=-1, keepdims=True)

    def pass_on(s, c):
        gx_copy(s, c).wait_recv()
        each(along - 1, lambda j: gy_copy(s, c, j + 1).start())

    def error_parts(s):
        lacc[...] = jnp.zeros_like(lacc)
        sum_along(s, 0)
        sum_along(s, 1)
        finish_error(s, 0)

        def middle(i):
            sum_along(s, i + 2)
            finish_error(s, i + 1)
            pass_on(s, i)

        each(CHUNKS - 2, middle)
        finish_error(s, CHUNKS - 1)
        pass_on(s, CHUNKS - 2)
        pass_on(s, CHUNKS - 1)
        lb[s, mine] = lacc[...] * (1.0 / dim)
        each(groups - 1, lambda j: ls_copy(s, j + 1).start())

    def grad_mixed_chunk(s, weight, c):
        each(along - 1, lambda j: gy_copy(s, c, j + 1).wait_recv())
        gm[...] = gm[...] + dotg(go[s, c], weight[:, window(c, width)], NT)

    def grad_values(s, weight):
        gm[...] = jnp.zeros_like(gm)
        each(CHUNKS, functools.partial(grad_mixed_chunk, s, weight))
        grad_mixed = weighted((gm[...] * out_scale).astype(BF), s)
        for h in range(heads):
            at = slice(h * HEAD, (h + 1) * HEAD)
            gw[:, at] = weighted_half(dotg(pb[s, h], grad_mixed[:, at], TN).astype(BF), s)

    def weighted_half(x, s):
        return (x.astype(F32) * cc[s, :, :HEAD]).astype(BF)

    def adam(grad, moment, second, old, peer, new, keep, at):
        g = grad
        first = beta_one * moment[at].astype(F32) + (1.0 - beta_one) * g
        square = beta_two * second[at].astype(F32) + (1.0 - beta_two) * g * g
        middle = 0.5 * (old[at].astype(F32) + peer[at].astype(F32))
        root = square * lax.rsqrt(square)
        updated = middle - learn_rate * (first / (root + epsilon) + decay_rate * middle)
        new[at] = updated.astype(BF)
        if keep:
            moment[at] = first.astype(BF)
            second[at] = square.astype(BF)

    def update_v_chunk(s, old, new, i):
        step = dim // CHUNKS
        gbv[...] = dot(nt[window(i, step), :], gw[...]) * in_scale

        def one(t):
            adam(gbv[window(t, 32), :], vmb, vvb, old, pv.at[s], new, s == 0, (pl.ds(pl.multiple_of(i * step + t * 32, 32), 32), slice(None)))

        each(step // 32, one, 2)

    def update_o_chunk(s, old, new, c):
        gbo[...] = dot(mt[s], go[s, c]) * out_scale

        def one(t):
            adam(gbo[window(t, tile), :], omb, ovb, old, po.at[s], new, s == 0, (window(t, tile), window(c, width)))

        each(inner // tile, one, 2)

    probabilities(0)
    loads["v"].wait()
    mix(0, v0)
    loads["o"].wait()
    each(CHUNKS, functools.partial(partial_chunk, 0, o0))
    probabilities(1)
    mix_turned(0)

    def turn(i):
        nt[window(i, rows), :] = nb[:, window(i, rows)].astype(F32).T.astype(BF)

    each(dim // rows, turn)
    loads["c"].wait()
    error_parts(0)
    if granted[0]:
        send_when_granted(0)
    forward(0, 0)
    forward(0, 1)
    grad_values(0, o0)
    if far:
        exchange_v(0).wait_send()
        exchange_o(0).start()
    for name in ("vm", "vv", "om", "ov"):
        loads[name].wait()
    arrived(0, 0)
    each(CHUNKS, functools.partial(update_v_chunk, 0, v0, v1))
    send(1, 0)

    mix(1, v1)
    arrived(0, 1)

    def next_chunk(c):
        update_o_chunk(0, o0, o1, c)
        partial_chunk(1, o1, c)

    each(CHUNKS, next_chunk)
    if not granted[1]:
        send(1, 1)
    mix_turned(1)
    error_parts(1)
    if granted[1]:
        send_when_granted(1)
    forward(1, 0)
    grad_values(1, o1)
    forward(1, 1)
    arrived(1, 0)

    def out_v(i):
        at = window(i, dim // CHUNKS)
        return pltpu.make_async_copy(v2.at[at, :], v_out.at[at, :], out_sem.at[0, i])

    def out_o(c):
        cols = window(c, width)
        return pltpu.make_async_copy(o2.at[:, cols], o_out.at[:, cols], out_sem.at[1, c])

    def last_v(i):
        update_v_chunk(1, v1, v2, i)
        out_v(i).start()

    each(CHUNKS, last_v)

    arrived(1, 1)

    def last_o(c):
        update_o_chunk(1, o1, o2, c)
        out_o(c).start()

    each(CHUNKS, last_o)

    share = loss_out.shape[1]
    for s in range(2):
        each(groups - 1, lambda j: ls_copy(s, j + 1).wait_recv())
        picked = jnp.sum(jnp.where(present(s), lb[s][:, 0:1], 0.0), axis=0, keepdims=True)
        chosen = jnp.zeros((1, share), F32)
        for g in range(groups):
            chosen = jnp.where(rank == g, picked[:, g * share : (g + 1) * share], chosen)
        loss_out[s : s + 1, :] = chosen

    for s in range(2):
        if split[s]:
            for which in range(2):
                first_leg(s, which).wait_send()
                second_leg(s, which).wait_send()
        exchange_o(s).wait_send()
        if s == 1 or not far:
            exchange_v(s).wait_send()

        def sent(c):
            each(along - 1, lambda j: ry_copy(s, c, j + 1).wait_send())
            rx_copy(s, c).wait_send()
            gx_copy(s, c).wait_send()
            each(along - 1, lambda j: gy_copy(s, c, j + 1).wait_send())

        each(CHUNKS, sent)
        each(groups - 1, lambda j: ls_copy(s, j + 1).wait_send())
    each(CHUNKS, lambda i: out_v(i).wait())
    each(CHUNKS, lambda c: out_o(c).wait())


def train(start, ids, gain, noisy, clean, q, k, v, o, vm, vv, om, ov):
    n_blk, groups = lax.axis_size("blk"), lax.axis_size("tp")
    rows, dim = noisy.shape
    inner = q.shape[1]
    width = dim // CHUNKS
    own = rows // groups
    vec = pl.BlockSpec(memory_space=pltpu.VMEM)
    hbm = pl.BlockSpec(memory_space=pl.ANY)
    V = pltpu.VMEM
    dma = pltpu.SemaphoreType.DMA
    tall, flat = V((dim, inner), BF), V((inner, dim), BF)
    return pl.pallas_call(
        functools.partial(kernel, start, n_blk, groups),
        out_shape=(
            jax.ShapeDtypeStruct(v.shape, BF),
            jax.ShapeDtypeStruct(o.shape, BF),
            jax.ShapeDtypeStruct((2, ids.shape[1] // groups), F32),
        ),
        in_specs=[vec, vec] + [hbm] * 10,
        out_specs=(hbm, hbm, vec),
        scratch_shapes=[
            V((rows, dim), BF),
            V((own, dim), BF),
            tall,
            tall,
            tall,
            flat,
            tall,
            flat,
            tall,
            flat,
            tall,
            tall,
            flat,
            flat,
            V((2, dim, inner), BF),
            V((2, inner, dim), BF),
            V((rows, dim), BF),
            V((dim, rows), BF),
            V((inner // HEAD, rows, rows), F32),
            V((2, inner // HEAD, rows, rows), BF),
            V((2, rows, inner), BF),
            V((2, inner, rows), BF),
            V((2, rows, inner), F32),
            V((rows, inner), F32),
            V((rows, inner), BF),
            V((dim // CHUNKS, inner), F32),
            V((inner, width), F32),
            V((own, 128), F32),
            V((2, CHUNKS, rows, width), BF),
            V((2, CHUNKS, groups // 2, 2 * own, width), BF),
            V((2, CHUNKS, own, width), BF),
            V((2, CHUNKS, own, width), BF),
            V((CHUNKS, own, width), F32),
            V((2, CHUNKS, rows, width), BF),
            V((2, rows, 128), F32),
            dma((10,)),
            dma((2, CHUNKS)),
            dma((2, 2)),
            dma((2, 2)),
            dma((2, CHUNKS, groups // 2)),
            dma((2, CHUNKS, groups // 2)),
            dma((2, CHUNKS)),
            dma((2, CHUNKS)),
            dma((2, CHUNKS)),
            dma((2, CHUNKS)),
            dma((2, CHUNKS, groups // 2)),
            dma((2, CHUNKS, groups // 2)),
            dma((2, groups)),
            dma((2, groups)),
            pltpu.SemaphoreType.REGULAR((2,)),
            dma((4,)),
            dma((4,)),
            V((dim // 4, inner), BF),
            V((inner, dim // 4), BF),
        ],
        compiler_params=pltpu.CompilerParams(
            collective_id=start, has_side_effects=True, vmem_limit_bytes=56 << 20
        ),
        cost_estimate=pl.CostEstimate(flops=3_200_000_000, bytes_accessed=12 << 20, transcendentals=0),
        name=f"train_{start}",
    )(ids, gain, noisy, clean, q, k, v, o, vm, vv, om, ov)


def on_device(step_index, patch_ids, noisy_pool, clean_pool, norm_gain, q_weight, k_weight, value_weight, out_weight, value_m, value_v, out_m, out_v):
    nbits = lax.axis_size("blk").bit_length() - 1
    return lax.switch(
        step_index[0] % nbits,
        [functools.partial(train, e) for e in range(nbits)],
        patch_ids[0],
        norm_gain[None, :],
        noisy_pool,
        clean_pool,
        q_weight,
        k_weight,
        value_weight,
        out_weight,
        value_m,
        value_v,
        out_m,
        out_v,
    )


def solution(mesh):
    in_specs = (
        P(),
        P("blk", None, None),
        P("blk", None),
        P("blk", None),
        P(),
        P(None, "tp"),
        P(None, "tp"),
        P("blk", "tp"),
        P(("blk", "tp"), None),
        P("blk", "tp"),
        P("blk", "tp"),
        P(("blk", "tp"), None),
        P(("blk", "tp"), None),
    )
    out_specs = (P("blk", "tp"), P(("blk", "tp"), None), P("blk", "tp"))
    return jax.shard_map(on_device, mesh=mesh, in_specs=in_specs, out_specs=out_specs, check_vma=False)
```
